512 devices in a mesh: mem: 64 (over x, y, core), patch: 8 (over z).
Axes of the slice: x: 4, y: 8, z: 8, core: 2. Of those that a mesh axis runs over, the one named last changes fastest.
Arguments:
- state: bfloat16 [3, 1024, 131072], P(None, 'mem', 'patch'), may hold values from -6 to 6
- obs_noise: bfloat16 [1024, 131072], P('mem', 'patch'), may hold values from -6 to 6
- obs_values: float32 [8, 16384], P('patch', 'mem'), may hold values from -6 to 6
- obs_weights: bfloat16 [8, 128, 128, 128], P('patch', 'mem'), may hold values from -1 to 1
- tapers: float32 [8, 128, 128], replicated, may hold values from 0.2 to 1
- pair_source: int32 [8, 128, 4], P('patch', 'mem'), may hold values from 0 to 127, as said below
- pair_taper: int32 [8, 128, 4], P('patch', 'mem'), may hold values from 0 to 7
Outputs:
- analysis: bfloat16 [3, 1024, 131072], P(None, 'mem', 'patch')
The draws below stay inside these ranges and needn't reach their ends.
Inputs may be any that keep to these rules, and one draw needn't show every extreme that they name: `pair_source`: each listed source lies in the same patch within 2 blocks of its target block; positions beyond the patch's ends are moved to its first or last block.
All inputs are finite; a program needn't handle non-finite values.
Results may differ from the reference program's by a relative error of at most 0.0058.
Values may be sent and summed in bfloat16 or wider, within the bound.
No kernel may reach another device: no remote copies, remote signals or barrier semaphores. Data moves between devices by JAX's collectives and lax.ppermute only.
A program may use at most 64 MiB of HBM per device.

```python
import jax
import jax.numpy as jnp
from jax import lax

MEMBERS = 1024
VARIABLES = 3
BLOCK_CELLS = 128
RADIUS = 2
PAIRS = 4
TAPERS = 8
PATCHES = 8
PATCH_BLOCKS = 128
PATCH_CELLS = 16384
TOTAL_CELLS = 131072


def draw_obs_weights(key, part):
    first_key, second_key = jax.random.split(jax.random.fold_in(key, 17))
    shape = (PATCHES, PATCH_BLOCKS, BLOCK_CELLS, BLOCK_CELLS)
    diagonal = jnp.exp(jax.random.uniform(first_key, shape[:3], jnp.float32, jnp.log(0.3), 0.0))
    spread = jax.random.normal(second_key, shape, jnp.float32)
    offdiag = jnp.clip(spread * 0.5 / jnp.sqrt(1.0 * BLOCK_CELLS), -0.3, 0.3)
    unit = jnp.eye(BLOCK_CELLS, dtype=jnp.float32)
    weights = offdiag * (1.0 - unit) + unit * diagonal[..., None]
    return weights.astype(jnp.bfloat16)


def draw_pair_source(key, part):
    width = 2 * RADIUS + 1
    scores = jax.random.randint(jax.random.fold_in(key, 29), (PATCHES, PATCH_BLOCKS, width), 0, 4096)
    scores = scores * 8 + jnp.arange(width, dtype=jnp.int32)
    order = jnp.argsort(scores, axis=-1, stable=True)[..., :PAIRS].astype(jnp.int32)
    target = jnp.arange(PATCH_BLOCKS, dtype=jnp.int32)[None, :, None]
    source = jnp.clip(target + order - RADIUS, 0, PATCH_BLOCKS - 1)
    return source.astype(jnp.int32)


def plant(drawn, own_key, smallest, high):
    extent = drawn.shape
    index_at = [jax.random.randint(jax.random.fold_in(own_key, axis), (), 0, extent[axis]) for axis in range(len(extent))]
    drawn = drawn.at[tuple(index_at)].set(smallest)
    longest = extent.index(max(extent))
    index_at[longest] = (index_at[longest] + 1) % extent[longest]
    return drawn.at[tuple(index_at)].set(high)


def shard_levels(own_key, shape, shards, least, top_value):
    loudness, own = 1.0, jax.random.fold_in(own_key, 6)
    for axis_at, parts in shards:
        heights = jnp.exp(jax.random.uniform(jax.random.fold_in(own, axis_at), (parts,), jnp.float32, least / len(shards), top_value / len(shards)))
        loudness = loudness * jnp.repeat(heights, shape[axis_at] // parts).reshape([-1 if axis == axis_at else 1 for axis in range(len(shape))])
    return loudness


def normal_values(own_key, dims, deviation, reach, cuts=(), held_as=jnp.bfloat16):
    entries = jax.random.normal(own_key, dims, jnp.float32) * deviation
    if len(cuts) > 0:
        entries = shard_levels(own_key, dims, cuts, -0.22, 0.18) * entries
    return jnp.clip(entries, min=-reach, max=reach).astype(held_as)


def setup_inputs(seed: int = 0) -> dict:
    arg_keys = jax.random.split(jax.random.key(seed), 8)
    state = normal_values(arg_keys[0], (VARIABLES, MEMBERS, TOTAL_CELLS), 1.0, 6.0, ((1, 64), (2, 8)))
    obs_noise = normal_values(arg_keys[1], (MEMBERS, TOTAL_CELLS), 1.0, 6.0, ((0, 64), (1, 8)))
    obs_values = normal_values(arg_keys[2], (PATCHES, PATCH_CELLS), 1.0, 6.0, ((0, 8), (1, 64)), jnp.float32)
    obs_weights = draw_obs_weights(jax.random.fold_in(arg_keys[7], 71), 0)
    tapers = jnp.clip(jax.random.uniform(arg_keys[4], (TAPERS, BLOCK_CELLS, BLOCK_CELLS), jnp.float32, 0.2, 1.0), 0.2, 1.0)
    pair_source = draw_pair_source(jax.random.fold_in(arg_keys[7], 71), 0)
    pair_taper = plant(jax.random.randint(arg_keys[6], (PATCHES, PATCH_BLOCKS, PAIRS), 0, TAPERS), jax.random.fold_in(arg_keys[6], 1), 0, TAPERS - 1).astype(jnp.int32)
    return {"state": state, "obs_noise": obs_noise, "obs_values": obs_values, "obs_weights": obs_weights, "tapers": tapers, "pair_source": pair_source, "pair_taper": pair_taper}


def reference(state, obs_noise, obs_values, obs_weights, tapers, pair_source, pair_taper):
    grid = state.reshape(VARIABLES, MEMBERS, PATCHES, PATCH_BLOCKS, BLOCK_CELLS).astype(jnp.float32)
    center = jnp.mean(grid, axis=1, keepdims=True)
    anomaly = (grid - center).astype(jnp.bfloat16)
    noise_grid = obs_noise.reshape(MEMBERS, PATCHES, PATCH_BLOCKS, BLOCK_CELLS).astype(jnp.float32)
    observed = obs_values.reshape(PATCHES, PATCH_BLOCKS, BLOCK_CELLS)
    innovation = (observed[None] + noise_grid - grid[0]).astype(jnp.bfloat16)
    weighted = jnp.einsum("pbcd,npbd->npbc", obs_weights.astype(jnp.float32),
                          innovation.astype(jnp.float32)).astype(jnp.bfloat16)

    def per_patch(patch):
        anom_patch = anomaly[:, :, patch]
        weight_patch = weighted[:, patch]
        source_patch = pair_source[patch]
        taper_patch = pair_taper[patch]

        def per_target(target):
            target_anom = anom_patch[:, :, target].astype(jnp.float32)
            total = jnp.zeros((VARIABLES, MEMBERS, BLOCK_CELLS), jnp.float32)
            for slot in range(PAIRS):
                source = source_patch[target, slot]
                source_anom = anom_patch[0, :, source].astype(jnp.float32)
                source_weight = weight_patch[:, source].astype(jnp.float32)
                taper = tapers[taper_patch[target, slot]]
                covariance = jnp.einsum("vnc,nd->vcd", target_anom, source_anom) / (MEMBERS - 1)
                localized = (taper * covariance).astype(jnp.bfloat16)
                total = total + jnp.einsum("nd,vcd->vnc", source_weight, localized.astype(jnp.float32))
            return total

        return lax.map(per_target, jnp.arange(PATCH_BLOCKS, dtype=jnp.int32))

    increment = lax.map(per_patch, jnp.arange(PATCHES, dtype=jnp.int32))
    increment = jnp.transpose(increment, (2, 3, 0, 1, 4)).reshape(VARIABLES, MEMBERS, TOTAL_CELLS)
    return (state.astype(jnp.float32) + increment).astype(jnp.bfloat16)
```

```python
import jax
import jax.numpy as jnp
from jax import lax
from jax.experimental import pallas as pl
from jax.experimental.pallas import tpu as pltpu
from jax.sharding import PartitionSpec as P

MEMBERS = 1024
VARIABLES = 3
BLOCK = 128
RADIUS = 2
PAIRS = 4
OWNED = 2
CELLS = OWNED * BLOCK
LOCAL_MEMBERS = 16
RING = 64
TILES = MEMBERS // BLOCK

VMEM = pl.BlockSpec(memory_space=pltpu.VMEM)
SMEM = pl.BlockSpec(memory_space=pltpu.SMEM)
PARAMS = pltpu.CompilerParams(vmem_limit_bytes=40 * 1024 * 1024)
BF16 = jnp.bfloat16
F32 = jnp.float32


def shape(*dims, dtype=BF16):
    return jax.ShapeDtypeStruct(dims, dtype)


def columns(ref, slot):
    return ref[:, slot].reshape(MEMBERS, CELLS)


def prepare_kernel(arrived, obs, weights, edges):
    first = columns(arrived, 0).astype(F32)
    noise = columns(arrived, 1).astype(F32)
    mean = jnp.sum(first, axis=0, keepdims=True) * (1.0 / MEMBERS)
    anomaly = (first - mean).astype(BF16)
    innovation = (obs[...] + noise - first).astype(BF16)
    for block in range(OWNED):
        lanes = slice(block * BLOCK, (block + 1) * BLOCK)
        edges[1, block] = lax.dot_general(
            innovation[:, lanes],
            weights[block],
            (((1,), (1,)), ((), ())),
            preferred_element_type=F32,
        ).astype(BF16)
        for tile in range(TILES):
            rows = slice(tile * BLOCK, (tile + 1) * BLOCK)
            edges[0, block, rows] = anomaly[rows, lanes].T


def source_rows(window, source):
    tiles = [window[0, source, tile * BLOCK : (tile + 1) * BLOCK] for tile in range(TILES)]
    return jnp.concatenate(tiles, axis=1)


def block_update(window, sums, tapers, index, block, values, count):
    wide, raw = values
    mean = jnp.sum(wide, axis=0, keepdims=True) * (1.0 / MEMBERS)
    sources = [index[block, pair] for pair in range(PAIRS)]
    left = jnp.concatenate([source_rows(window, s) for s in sources], axis=0)
    covariance = jnp.dot(left, raw, preferred_element_type=F32)
    pieces = []
    for pair in range(PAIRS):
        part = covariance[pair * BLOCK : (pair + 1) * BLOCK]
        part = part - sums[sources[pair]][:, :1] * mean
        taper = tapers[block, pair]
        pieces.append((part * jnp.concatenate([taper] * count, axis=1)).astype(BF16))
    localized = jnp.concatenate(pieces, axis=0)
    weighted = jnp.concatenate([window[1, s] for s in sources], axis=1)
    return wide + jnp.dot(weighted, localized, preferred_element_type=F32)


def first_kernel(index, taper_at, before, middle, after, arrived, table, window, sums, tapers, out):
    for place, part in enumerate((before, middle, after)):
        for kind in range(2):
            window[kind, place * OWNED : (place + 1) * OWNED] = part[kind]
    for source in range(3 * OWNED):
        total = jnp.sum(source_rows(window, source).astype(F32), axis=1, keepdims=True)
        sums[source] = jnp.broadcast_to(total, (BLOCK, BLOCK))
    for block in range(OWNED):
        for pair in range(PAIRS):
            tapers[block, pair] = table[taper_at[block, pair]].T * (1.0 / (MEMBERS - 1))
    for block in range(OWNED):
        lanes = slice(block * BLOCK, (block + 1) * BLOCK)
        raw = arrived[:, 0, :, lanes].reshape(MEMBERS, BLOCK)
        result = block_update(window, sums, tapers, index, block, (raw.astype(F32), raw), 1)
        out[:, :, lanes] = result.astype(BF16).reshape(RING, LOCAL_MEMBERS, BLOCK)


def rest_kernel(index, window, sums, tapers, arrived, first, out):
    out[:, 0] = first[...]
    for block in range(OWNED):
        lanes = slice(block * BLOCK, (block + 1) * BLOCK)
        raw = jnp.concatenate(
            [arrived[:, v, :, lanes].reshape(MEMBERS, BLOCK) for v in range(2)], axis=1
        )
        result = block_update(window, sums, tapers, index, block, (raw.astype(F32), raw), 2)
        for v in range(2):
            part = result[:, v * BLOCK : (v + 1) * BLOCK].astype(BF16)
            out[:, 1 + v, :, lanes] = part.reshape(RING, LOCAL_MEMBERS, BLOCK)


def pack_kernel(*refs):
    sources, out = refs[:-1], refs[-1]
    for slot, ref in enumerate(sources):
        for owner in range(RING):
            out[owner, slot] = ref[:, owner * CELLS : (owner + 1) * CELLS]


def pack(*arrays):
    count = len(arrays)
    return pl.pallas_call(
        pack_kernel,
        out_shape=shape(RING, count, LOCAL_MEMBERS, CELLS),
        in_specs=[VMEM] * count,
        out_specs=VMEM,
        compiler_params=PARAMS,
    )(*arrays)


def exchange(packed):
    return lax.all_to_all(packed, "mem", split_axis=0, concat_axis=0, tiled=True)


def on_device(state, obs_noise, obs_values, obs_weights, tapers, pair_source, pair_taper):
    arrived = exchange(pack(state[0], obs_noise))
    others = exchange(pack(state[1], state[2]))
    edges = pl.pallas_call(
        prepare_kernel,
        out_shape=shape(2, OWNED, MEMBERS, BLOCK),
        in_specs=[VMEM] * 3,
        out_specs=VMEM,
        compiler_params=PARAMS,
    )(arrived, obs_values, obs_weights[0])
    ends = RING - 1
    before = lax.ppermute(edges, "mem", [(i, i + 1) for i in range(ends)])
    after = lax.ppermute(edges, "mem", [(i + 1, i) for i in range(ends)])
    index = pair_source[0] - (lax.axis_index("mem") * OWNED - RADIUS)
    window, sums, taper_tiles, first = pl.pallas_call(
        first_kernel,
        out_shape=(
            shape(2, 3 * OWNED, MEMBERS, BLOCK),
            shape(3 * OWNED, BLOCK, BLOCK, dtype=F32),
            shape(OWNED, PAIRS, BLOCK, BLOCK, dtype=F32),
            shape(RING, LOCAL_MEMBERS, CELLS),
        ),
        in_specs=[SMEM, SMEM] + [VMEM] * 5,
        out_specs=(VMEM,) * 4,
        compiler_params=PARAMS,
    )(index, pair_taper[0], before, edges, after, arrived, tapers)
    updated = pl.pallas_call(
        rest_kernel,
        out_shape=shape(RING, VARIABLES, LOCAL_MEMBERS, CELLS),
        in_specs=[SMEM] + [VMEM] * 5,
        out_specs=VMEM,
        compiler_params=PARAMS,
    )(index, window, sums, taper_tiles, others, first)
    back = exchange(updated)
    return jnp.transpose(back, (1, 2, 0, 3)).reshape(VARIABLES, LOCAL_MEMBERS, RING * CELLS)


def solution(mesh):
    placed = (
        P(None, "mem", "patch"),
        P("mem", "patch"),
        P("patch", "mem"),
        P("patch", "mem", None, None),
        P(),
        P("patch", "mem", None),
        P("patch", "mem", None),
    )
    return jax.shard_map(
        on_device, mesh=mesh, in_specs=placed, out_specs=P(None, "mem", "patch"), check_vma=False
    )
```

```python
import jax
import jax.numpy as jnp
from jax import lax
from jax.experimental import pallas as pl
from jax.experimental.pallas import tpu as pltpu
from jax.sharding import PartitionSpec as P

MEMBERS = 1024
VARIABLES = 3
BLOCK = 128
RADIUS = 2
PAIRS = 4
OWNED = 2
CELLS = OWNED * BLOCK
LOCAL_MEMBERS = 16
RING = 64
TILES = MEMBERS // BLOCK
PIECES = 4

VMEM = pl.BlockSpec(memory_space=pltpu.VMEM)
SMEM = pl.BlockSpec(memory_space=pltpu.SMEM)
HBM = pl.BlockSpec(memory_space=pltpu.HBM)
PARAMS = pltpu.CompilerParams(vmem_limit_bytes=40 * 1024 * 1024)
BF16 = jnp.bfloat16
F32 = jnp.float32


def shape(*dims, dtype=BF16):
    return jax.ShapeDtypeStruct(dims, dtype)


def prepare_kernel(arrived, obs, weights, edges):
    first = arrived[:, 0].reshape(MEMBERS, CELLS).astype(F32)
    noise = arrived[:, VARIABLES].reshape(MEMBERS, CELLS).astype(F32)
    mean = jnp.sum(first, axis=0, keepdims=True) * (1.0 / MEMBERS)
    anomaly = (first - mean).astype(BF16)
    innovation = (obs[...] + noise - first).astype(BF16)
    for block in range(OWNED):
        lanes = slice(block * BLOCK, (block + 1) * BLOCK)
        edges[1, block] = lax.dot_general(
            innovation[:, lanes],
            weights[block],
            (((1,), (1,)), ((), ())),
            preferred_element_type=F32,
        ).astype(BF16)
        for tile in range(TILES):
            rows = slice(tile * BLOCK, (tile + 1) * BLOCK)
            edges[0, block, rows] = anomaly[rows, lanes].T


def source_rows(window, source):
    tiles = [window[0, source, tile * BLOCK : (tile + 1) * BLOCK] for tile in range(TILES)]
    return jnp.concatenate(tiles, axis=1)


def center_kernel(arrived, centered):
    for variable in range(VARIABLES):
        wide = arrived[:, variable].reshape(MEMBERS, CELLS).astype(F32)
        mean = jnp.sum(wide, axis=0, keepdims=True) * (1.0 / MEMBERS)
        anomaly = (wide - mean).astype(BF16)
        for block in range(OWNED):
            lanes = slice(block * BLOCK, (block + 1) * BLOCK)
            centered[block, :, variable * BLOCK : (variable + 1) * BLOCK] = anomaly[:, lanes]


def taper_kernel(taper_at, table, tapers):
    for block in range(OWNED):
        for pair in range(PAIRS):
            tile = table[taper_at[block, pair]].T * (1.0 / (MEMBERS - 1))
            tapers[block, pair * BLOCK : (pair + 1) * BLOCK] = tile


def window_copies(parts, window, sems):
    copies = []
    for kind in range(2):
        for place, part in enumerate(parts):
            copies.append(
                pltpu.make_async_copy(
                    part.at[kind],
                    window.at[kind, pl.ds(place * OWNED, OWNED)],
                    sems.at[kind * 3 + place],
                )
            )
    return copies[:3], copies[3:]


def update_kernel(
    index, before, middle, after, arrived, centered, tapers, updated, window, out, sems
):
    anomalies, weighted = window_copies((before, middle, after), window, sems)
    for copy in anomalies + weighted:
        copy.start()
    sources = [[index[block, pair] for pair in range(PAIRS)] for block in range(OWNED)]
    for copy in anomalies:
        copy.wait()
    localized = []
    for block in range(OWNED):
        left = jnp.concatenate([source_rows(window, s) for s in sources[block]], axis=0)
        covariance = jnp.dot(left, centered[block], preferred_element_type=F32)
        taper = jnp.concatenate([tapers[block]] * VARIABLES, axis=1)
        localized.append((taper * covariance).astype(BF16))
    for copy in weighted:
        copy.wait()
    depth, owners = MEMBERS // PIECES, RING // PIECES
    leaving = []
    for piece in range(PIECES):
        rows = slice(piece * depth, (piece + 1) * depth)
        held = slice(piece * owners, (piece + 1) * owners)
        for block in range(OWNED):
            lanes = slice(block * BLOCK, (block + 1) * BLOCK)
            right = jnp.concatenate([window[1, s, rows] for s in sources[block]], axis=1)
            step = jnp.dot(right, localized[block], preferred_element_type=F32)
            for v in range(VARIABLES):
                base = arrived[held, v, :, lanes].reshape(depth, BLOCK).astype(F32)
                result = base + step[:, v * BLOCK : (v + 1) * BLOCK]
                out[held, v, :, lanes] = result.astype(BF16).reshape(owners, LOCAL_MEMBERS, BLOCK)
        part = pl.ds(piece * owners, owners)
        copy = pltpu.make_async_copy(out.at[part], updated.at[part], sems.at[6 + piece])
        copy.start()
        leaving.append(copy)
    for copy in leaving:
        copy.wait()


def pack_kernel(slots, *refs):
    count = len(slots)
    sources, out, held, sems = refs[: count], refs[count], refs[count + 1], refs[count + 2]
    width = RING * CELLS // PIECES
    copies = []
    for piece in range(PIECES):
        for slot, ref in enumerate(sources):
            lanes = pl.ds(piece * width, width)
            source = ref.at[:, lanes] if slots[slot] is None else ref.at[slots[slot], :, lanes]
            copies.append(
                pltpu.make_async_copy(
                    source, held.at[slot, :, lanes], sems.at[piece * count + slot]
                )
            )
    for copy in copies:
        copy.start()
    each = RING // PIECES
    for piece in range(PIECES):
        for slot in range(count):
            copies[piece * count + slot].wait()
            for rank in range(piece * each, (piece + 1) * each):
                lanes = slice(rank * CELLS, (rank + 1) * CELLS)
                out[rank, slot] = held[slot, :, lanes]


def pack(*arrays):
    count = len(arrays)

    def kernel(*refs):
        pack_kernel([slot for _, slot in arrays], *refs)

    return pl.pallas_call(
        kernel,
        out_shape=pltpu.HBM((RING, count, LOCAL_MEMBERS, CELLS), BF16),
        in_specs=[HBM] * count,
        out_specs=VMEM,
        scratch_shapes=[
            pltpu.VMEM((count, LOCAL_MEMBERS, RING * CELLS), BF16),
            pltpu.SemaphoreType.DMA((PIECES * count,)),
        ],
        compiler_params=PARAMS,
    )(*[in_hbm(array) for array, _ in arrays])


def unpack_kernel(back, out, held, sems):
    width, each = RING * CELLS // PIECES, RING // PIECES
    copies = []
    for piece in range(PIECES):
        for rank in range(piece * each, (piece + 1) * each):
            held[:, :, rank * CELLS : (rank + 1) * CELLS] = back[rank]
        lanes = pl.ds(piece * width, width)
        copy = pltpu.make_async_copy(held.at[:, :, lanes], out.at[:, :, lanes], sems.at[piece])
        copy.start()
        copies.append(copy)
    for copy in copies:
        copy.wait()


def unpack(back):
    return pl.pallas_call(
        unpack_kernel,
        out_shape=pltpu.HBM((VARIABLES, LOCAL_MEMBERS, RING * CELLS), BF16),
        in_specs=[VMEM],
        out_specs=HBM,
        scratch_shapes=[
            pltpu.VMEM((VARIABLES, LOCAL_MEMBERS, RING * CELLS), BF16),
            pltpu.SemaphoreType.DMA((PIECES,)),
        ],
        compiler_params=PARAMS,
    )(back)


def in_hbm(array):
    return pltpu.with_memory_space_constraint(array, pltpu.HBM)


def exchange(packed):
    return lax.all_to_all(packed, "mem", split_axis=0, concat_axis=0, tiled=True)


def on_device(state, obs_noise, obs_values, obs_weights, tapers, pair_source, pair_taper):
    arrived = exchange(pack((state, 0), (state, 1), (state, 2), (obs_noise, None)))
    edges = pl.pallas_call(
        prepare_kernel,
        out_shape=shape(2, OWNED, MEMBERS, BLOCK),
        in_specs=[VMEM] * 3,
        out_specs=VMEM,
        compiler_params=PARAMS,
    )(arrived, obs_values, obs_weights[0])
    ends = RING - 1
    before = lax.ppermute(edges, "mem", [(i, i + 1) for i in range(ends)])
    after = lax.ppermute(edges, "mem", [(i + 1, i) for i in range(ends)])
    centered = pl.pallas_call(
        center_kernel,
        out_shape=shape(OWNED, MEMBERS, VARIABLES * BLOCK),
        in_specs=[VMEM],
        out_specs=VMEM,
        compiler_params=PARAMS,
    )(arrived)
    taper_tiles = pl.pallas_call(
        taper_kernel,
        out_shape=shape(OWNED, PAIRS * BLOCK, BLOCK, dtype=F32),
        in_specs=[SMEM, VMEM],
        out_specs=VMEM,
        compiler_params=PARAMS,
    )(pair_taper[0], tapers)
    index = pair_source[0] - (lax.axis_index("mem") * OWNED - RADIUS)
    updated = pl.pallas_call(
        update_kernel,
        out_shape=pltpu.HBM((RING, VARIABLES, LOCAL_MEMBERS, CELLS), BF16),
        in_specs=[SMEM] + [HBM] * 3 + [VMEM] * 3,
        out_specs=HBM,
        scratch_shapes=[
            pltpu.VMEM((2, 3 * OWNED, MEMBERS, BLOCK), BF16),
            pltpu.VMEM((RING, VARIABLES, LOCAL_MEMBERS, CELLS), BF16),
            pltpu.SemaphoreType.DMA((6 + PIECES,)),
        ],
        compiler_params=PARAMS,
    )(index, in_hbm(before), in_hbm(edges), in_hbm(after), arrived, centered, taper_tiles)
    return unpack(exchange(updated))


def solution(mesh):
    placed = (
        P(None, "mem", "patch"),
        P("mem", "patch"),
        P("patch", "mem"),
        P("patch", "mem", None, None),
        P(),
        P("patch", "mem", None),
        P("patch", "mem", None),
    )
    return jax.shard_map(
        on_device, mesh=mesh, in_specs=placed, out_specs=P(None, "mem", "patch"), check_vma=False
    )
```

```python
import jax
import jax.numpy as jnp
from jax import lax
from jax.experimental import pallas as pl
from jax.experimental.pallas import tpu as pltpu
from jax.sharding import PartitionSpec as P

MEMBERS = 1024
VARIABLES = 3
BLOCK = 128
RADIUS = 2
PAIRS = 4
OWNED = 2
CELLS = OWNED * BLOCK
LOCAL_MEMBERS = 16
RING = 64
TILES = MEMBERS // BLOCK
PIECES = 4

VMEM = pl.BlockSpec(memory_space=pltpu.VMEM)
SMEM = pl.BlockSpec(memory_space=pltpu.SMEM)
HBM = pl.BlockSpec(memory_space=pltpu.HBM)
PARAMS = pltpu.CompilerParams(vmem_limit_bytes=40 * 1024 * 1024)
BF16 = jnp.bfloat16
F32 = jnp.float32


def shape(*dims, dtype=BF16):
    return jax.ShapeDtypeStruct(dims, dtype)


def prepare_kernel(arrived, obs, weights, tapers, anomalies, weighted):
    del tapers
    first = arrived[:, 0].reshape(MEMBERS, CELLS).astype(F32)
    noise = arrived[:, VARIABLES].reshape(MEMBERS, CELLS).astype(F32)
    mean = jnp.sum(first, axis=0, keepdims=True) * (1.0 / MEMBERS)
    anomaly = (first - mean).astype(BF16)
    innovation = (obs[...] + noise - first).astype(BF16)
    for block in range(OWNED):
        lanes = slice(block * BLOCK, (block + 1) * BLOCK)
        for tile in range(TILES):
            rows = slice(tile * BLOCK, (tile + 1) * BLOCK)
            anomalies[block, rows] = anomaly[rows, lanes].T
        weighted[block] = lax.dot_general(
            innovation[:, lanes],
            weights[block],
            (((1,), (1,)), ((), ())),
            preferred_element_type=F32,
        ).astype(BF16)


def source_rows(window, source):
    tiles = [window[source, tile * BLOCK : (tile + 1) * BLOCK] for tile in range(TILES)]
    return jnp.concatenate(tiles, axis=1)


def center_kernel(arrived, centered):
    for variable in range(VARIABLES):
        wide = arrived[:, variable].reshape(MEMBERS, CELLS).astype(F32)
        mean = jnp.sum(wide, axis=0, keepdims=True) * (1.0 / MEMBERS)
        anomaly = (wide - mean).astype(BF16)
        for block in range(OWNED):
            lanes = slice(block * BLOCK, (block + 1) * BLOCK)
            centered[block, :, variable * BLOCK : (variable + 1) * BLOCK] = anomaly[:, lanes]


def taper_kernel(taper_at, table, tapers):
    for block in range(OWNED):
        for pair in range(PAIRS):
            tile = table[taper_at[block, pair]].T * (1.0 / (MEMBERS - 1))
            tapers[block, pair * BLOCK : (pair + 1) * BLOCK] = tile


def localize_kernel(index, across, own, mate, centered, tapers, localized, window):
    window[:OWNED] = across[...]
    window[OWNED : 2 * OWNED] = own[...]
    window[2 * OWNED :] = mate[...]
    for block in range(OWNED):
        sources = [index[block, pair] for pair in range(PAIRS)]
        left = jnp.concatenate([source_rows(window, s) for s in sources], axis=0)
        covariance = jnp.dot(left, centered[block], preferred_element_type=F32)
        taper = jnp.concatenate([tapers[block]] * VARIABLES, axis=1)
        localized[block] = (taper * covariance).astype(BF16)


def update_kernel(index, across, own, mate, arrived, localized, updated, window, out, out_sems):
    depth, owners = MEMBERS // PIECES, RING // PIECES
    sources = [[index[block, pair] for pair in range(PAIRS)] for block in range(OWNED)]
    leaving = []
    for piece in range(PIECES):
        rows = slice(piece * depth, (piece + 1) * depth)
        held = slice(piece * owners, (piece + 1) * owners)
        window[:OWNED, rows] = across[:, rows]
        window[OWNED : 2 * OWNED, rows] = own[:, rows]
        window[2 * OWNED :, rows] = mate[:, rows]
        for block in range(OWNED):
            lanes = slice(block * BLOCK, (block + 1) * BLOCK)
            right = jnp.concatenate([window[s, rows] for s in sources[block]], axis=1)
            step = jnp.dot(right, localized[block], preferred_element_type=F32)
            for v in range(VARIABLES):
                base = arrived[held, v, :, lanes].reshape(depth, BLOCK).astype(F32)
                result = base + step[:, v * BLOCK : (v + 1) * BLOCK]
                out[held, v, :, lanes] = result.astype(BF16).reshape(owners, LOCAL_MEMBERS, BLOCK)
        part = pl.ds(piece * owners, owners)
        copy = pltpu.make_async_copy(out.at[part], updated.at[part], out_sems.at[piece])
        copy.start()
        leaving.append(copy)
    for copy in leaving:
        copy.wait()


def pack_kernel(state, noise, packed, held, out, sems, out_sems):
    width, each = RING * CELLS // PIECES, RING // PIECES
    entering = []
    for piece in range(PIECES):
        lanes = pl.ds(piece * width, width)
        pair = (
            pltpu.make_async_copy(
                state.at[:, :, lanes], held.at[pl.ds(0, VARIABLES), :, lanes], sems.at[2 * piece]
            ),
            pltpu.make_async_copy(
                noise.at[:, lanes], held.at[VARIABLES, :, lanes], sems.at[2 * piece + 1]
            ),
        )
        for copy in pair:
            copy.start()
        entering.append(pair)
    leaving = []
    for piece in range(PIECES):
        for copy in entering[piece]:
            copy.wait()
        for rank in range(piece * each, (piece + 1) * each):
            out[rank] = held[:, :, rank * CELLS : (rank + 1) * CELLS]
        part = pl.ds(piece * each, each)
        copy = pltpu.make_async_copy(out.at[part], packed.at[part], out_sems.at[piece])
        copy.start()
        leaving.append(copy)
    for copy in leaving:
        copy.wait()


def pack(state, noise):
    count = VARIABLES + 1
    return pl.pallas_call(
        pack_kernel,
        out_shape=pltpu.HBM((RING, count, LOCAL_MEMBERS, CELLS), BF16),
        in_specs=[HBM] * 2,
        out_specs=HBM,
        scratch_shapes=[
            pltpu.VMEM((count, LOCAL_MEMBERS, RING * CELLS), BF16),
            pltpu.VMEM((RING, count, LOCAL_MEMBERS, CELLS), BF16),
            pltpu.SemaphoreType.DMA((2 * PIECES,)),
            pltpu.SemaphoreType.DMA((PIECES,)),
        ],
        compiler_params=PARAMS,
    )(in_hbm(state), in_hbm(noise))


def unpack_kernel(back, out, held, sems):
    width, each = RING * CELLS // PIECES, RING // PIECES
    copies = []
    for piece in range(PIECES):
        for rank in range(piece * each, (piece + 1) * each):
            held[:, :, rank * CELLS : (rank + 1) * CELLS] = back[rank]
        lanes = pl.ds(piece * width, width)
        copy = pltpu.make_async_copy(held.at[:, :, lanes], out.at[:, :, lanes], sems.at[piece])
        copy.start()
        copies.append(copy)
    for copy in copies:
        copy.wait()


def unpack(back):
    return pl.pallas_call(
        unpack_kernel,
        out_shape=pltpu.HBM((VARIABLES, LOCAL_MEMBERS, RING * CELLS), BF16),
        in_specs=[VMEM],
        out_specs=HBM,
        scratch_shapes=[
            pltpu.VMEM((VARIABLES, LOCAL_MEMBERS, RING * CELLS), BF16),
            pltpu.SemaphoreType.DMA((PIECES,)),
        ],
        compiler_params=PARAMS,
    )(back)


def in_hbm(array):
    return pltpu.with_memory_space_constraint(array, pltpu.HBM)


def exchange(packed):
    return lax.all_to_all(packed, "mem", split_axis=0, concat_axis=0, tiled=True)


def on_device(state, obs_noise, obs_values, obs_weights, tapers, pair_source, pair_taper):
    arrived = exchange(pack(state, obs_noise))
    half = (OWNED, MEMBERS, BLOCK)
    taper_tiles = pl.pallas_call(
        taper_kernel,
        out_shape=shape(OWNED, PAIRS * BLOCK, BLOCK, dtype=F32),
        in_specs=[SMEM, VMEM],
        out_specs=VMEM,
        compiler_params=PARAMS,
    )(pair_taper[0], tapers)
    anomalies, weighted = pl.pallas_call(
        prepare_kernel,
        out_shape=(shape(*half), shape(*half)),
        in_specs=[VMEM] * 4,
        out_specs=(VMEM,) * 2,
        compiler_params=PARAMS,
    )(arrived, obs_values, obs_weights[0], taper_tiles)
    across = [(i, i + 1) for i in range(1, RING - 1, 2)]
    across += [(j, i) for i, j in across]
    inside = [(i, i ^ 1) for i in range(RING)]
    across_anomalies = lax.ppermute(anomalies, "mem", across)
    across_weighted = lax.ppermute(weighted, "mem", across)
    centered = pl.pallas_call(
        center_kernel,
        out_shape=shape(OWNED, MEMBERS, VARIABLES * BLOCK),
        in_specs=[VMEM],
        out_specs=VMEM,
        compiler_params=PARAMS,
    )(arrived)
    mate_anomalies = lax.ppermute(anomalies, "mem", inside)
    mate_weighted = lax.ppermute(weighted, "mem", inside)
    place = lax.axis_index("mem")
    index = pair_source[0] - (place * OWNED - RADIUS)
    turn = jnp.where(place % 2 == 1, 2 * OWNED, 0)
    index = jnp.where(index < OWNED, index + turn, jnp.where(index < 2 * OWNED, index, index - turn))
    window = pltpu.VMEM((3 * OWNED, MEMBERS, BLOCK), BF16)
    localized = pl.pallas_call(
        localize_kernel,
        out_shape=shape(OWNED, PAIRS * BLOCK, VARIABLES * BLOCK),
        in_specs=[SMEM] + [VMEM] * 5,
        out_specs=VMEM,
        scratch_shapes=[window],
        compiler_params=PARAMS,
    )(index, across_anomalies, anomalies, mate_anomalies, centered, taper_tiles)
    updated = pl.pallas_call(
        update_kernel,
        out_shape=pltpu.HBM((RING, VARIABLES, LOCAL_MEMBERS, CELLS), BF16),
        in_specs=[SMEM] + [VMEM] * 5,
        out_specs=HBM,
        scratch_shapes=[
            window,
            pltpu.VMEM((RING, VARIABLES, LOCAL_MEMBERS, CELLS), BF16),
            pltpu.SemaphoreType.DMA((PIECES,)),
        ],
        compiler_params=PARAMS,
    )(index, across_weighted, weighted, mate_weighted, arrived, localized)
    return unpack(exchange(updated))


def solution(mesh):
    placed = (
        P(None, "mem", "patch"),
        P("mem", "patch"),
        P("patch", "mem"),
        P("patch", "mem", None, None),
        P(),
        P("patch", "mem", None),
        P("patch", "mem", None),
    )
    return jax.shard_map(
        on_device, mesh=mesh, in_specs=placed, out_specs=P(None, "mem", "patch"), check_vma=False
    )
```

```python
import jax
import jax.numpy as jnp
from jax import lax
from jax.experimental import pallas as pl
from jax.experimental.pallas import tpu as pltpu
from jax.sharding import PartitionSpec as P

MEMBERS = 1024
VARIABLES = 3
BLOCK = 128
RADIUS = 2
PAIRS = 4
OWNED = 2
CELLS = OWNED * BLOCK
LOCAL_MEMBERS = 16
RING = 64
TILES = MEMBERS // BLOCK
PIECES = 4

VMEM = pl.BlockSpec(memory_space=pltpu.VMEM)
SMEM = pl.BlockSpec(memory_space=pltpu.SMEM)
HBM = pl.BlockSpec(memory_space=pltpu.HBM)
PARAMS = pltpu.CompilerParams(vmem_limit_bytes=40 * 1024 * 1024)
BF16 = jnp.bfloat16
F32 = jnp.float32


def shape(*dims, dtype=BF16):
    return jax.ShapeDtypeStruct(dims, dtype)


def prepare_kernel(arrived, obs, weights, tapers, edges, anomalies, weighted):
    del tapers
    first = arrived[:, 0].reshape(MEMBERS, CELLS).astype(F32)
    noise = arrived[:, VARIABLES].reshape(MEMBERS, CELLS).astype(F32)
    mean = jnp.sum(first, axis=0, keepdims=True) * (1.0 / MEMBERS)
    anomaly = (first - mean).astype(BF16)
    innovation = (obs[...] + noise - first).astype(BF16)
    for block in range(OWNED):
        lanes = slice(block * BLOCK, (block + 1) * BLOCK)
        for tile in range(TILES):
            rows = slice(tile * BLOCK, (tile + 1) * BLOCK)
            turned = anomaly[rows, lanes].T
            edges[0, block, rows] = turned
            anomalies[block, rows] = turned
        product = lax.dot_general(
            innovation[:, lanes],
            weights[block],
            (((1,), (1,)), ((), ())),
            preferred_element_type=F32,
        ).astype(BF16)
        edges[1, block] = product
        weighted[block] = product


def member_columns(part, block):
    return jnp.concatenate(
        [part[block, tile * BLOCK : (tile + 1) * BLOCK] for tile in range(TILES)], axis=1
    )


def center_kernel(arrived, centered):
    for variable in range(VARIABLES):
        wide = arrived[:, variable].reshape(MEMBERS, CELLS).astype(F32)
        mean = jnp.sum(wide, axis=0, keepdims=True) * (1.0 / MEMBERS)
        anomaly = (wide - mean).astype(BF16)
        for block in range(OWNED):
            lanes = slice(block * BLOCK, (block + 1) * BLOCK)
            centered[block, :, variable * BLOCK : (variable + 1) * BLOCK] = anomaly[:, lanes]


def taper_kernel(index, taper_at, table, tapers):
    for block in range(OWNED):
        tiles = [table[taper_at[block, pair]].T * (1.0 / (MEMBERS - 1)) for pair in range(PAIRS)]
        for source in range(3 * OWNED):
            total = jnp.zeros((BLOCK, BLOCK), F32)
            for pair in range(PAIRS):
                total += tiles[pair] * jnp.where(index[block, pair] == source, 1.0, 0.0)
            tapers[block, source * BLOCK : (source + 1) * BLOCK] = total


def localized_part(left, centered, tapers):
    covariance = jnp.dot(left, centered, preferred_element_type=F32)
    return (jnp.concatenate([tapers] * VARIABLES, axis=1) * covariance).astype(BF16)


def near_kernel(own, mate, own_weighted, mate_weighted, centered, tapers, arrived, partial):
    depth, owners = MEMBERS // PIECES, RING // PIECES
    left = jnp.concatenate(
        [member_columns(part, block) for part in (own, mate) for block in range(OWNED)], axis=0
    )
    localized = [
        localized_part(left, centered[block], tapers[block, OWNED * BLOCK :])
        for block in range(OWNED)
    ]
    for piece in range(PIECES):
        rows = slice(piece * depth, (piece + 1) * depth)
        held = slice(piece * owners, (piece + 1) * owners)
        right = jnp.concatenate(
            [part[b, rows] for part in (own_weighted, mate_weighted) for b in range(OWNED)], axis=1
        )
        for block in range(OWNED):
            lanes = slice(block * BLOCK, (block + 1) * BLOCK)
            step = jnp.dot(right, localized[block], preferred_element_type=F32)
            for v in range(VARIABLES):
                base = arrived[held, v, :, lanes].reshape(depth, BLOCK).astype(F32)
                columns = slice(v * BLOCK, (v + 1) * BLOCK)
                partial[block, rows, columns] = base + step[:, columns]


def far_kernel(across, centered, tapers, partial, updated, out, out_sems):
    depth, owners = MEMBERS // PIECES, RING // PIECES
    leaving = []
    left = jnp.concatenate([member_columns(across.at[0], b) for b in range(OWNED)], axis=0)
    localized = [
        localized_part(left, centered[block], tapers[block, : OWNED * BLOCK])
        for block in range(OWNED)
    ]
    for piece in range(PIECES):
        rows = slice(piece * depth, (piece + 1) * depth)
        held = slice(piece * owners, (piece + 1) * owners)
        right = jnp.concatenate([across[1, block, rows] for block in range(OWNED)], axis=1)
        for block in range(OWNED):
            lanes = slice(block * BLOCK, (block + 1) * BLOCK)
            step = jnp.dot(right, localized[block], preferred_element_type=F32)
            result = (partial[block, rows] + step).astype(BF16)
            for v in range(VARIABLES):
                columns = slice(v * BLOCK, (v + 1) * BLOCK)
                out[held, v, :, lanes] = result[:, columns].reshape(owners, LOCAL_MEMBERS, BLOCK)
        part = pl.ds(piece * owners, owners)
        copy = pltpu.make_async_copy(out.at[part], updated.at[part], out_sems.at[piece])
        copy.start()
        leaving.append(copy)
    for copy in leaving:
        copy.wait()


def pack_kernel(state, noise, packed, held, out, sems, out_sems):
    width, each = RING * CELLS // PIECES, RING // PIECES
    entering = []
    for piece in range(PIECES):
        lanes = pl.ds(piece * width, width)
        pair = (
            pltpu.make_async_copy(
                state.at[:, :, lanes], held.at[pl.ds(0, VARIABLES), :, lanes], sems.at[2 * piece]
            ),
            pltpu.make_async_copy(
                noise.at[:, lanes], held.at[VARIABLES, :, lanes], sems.at[2 * piece + 1]
            ),
        )
        for copy in pair:
            copy.start()
        entering.append(pair)
    leaving = []
    for piece in range(PIECES):
        for copy in entering[piece]:
            copy.wait()
        for rank in range(piece * each, (piece + 1) * each):
            out[rank] = held[:, :, rank * CELLS : (rank + 1) * CELLS]
        part = pl.ds(piece * each, each)
        copy = pltpu.make_async_copy(out.at[part], packed.at[part], out_sems.at[piece])
        copy.start()
        leaving.append(copy)
    for copy in leaving:
        copy.wait()


def pack(state, noise):
    count = VARIABLES + 1
    return pl.pallas_call(
        pack_kernel,
        out_shape=pltpu.HBM((RING, count, LOCAL_MEMBERS, CELLS), BF16),
        in_specs=[HBM] * 2,
        out_specs=HBM,
        scratch_shapes=[
            pltpu.VMEM((count, LOCAL_MEMBERS, RING * CELLS), BF16),
            pltpu.VMEM((RING, count, LOCAL_MEMBERS, CELLS), BF16),
            pltpu.SemaphoreType.DMA((2 * PIECES,)),
            pltpu.SemaphoreType.DMA((PIECES,)),
        ],
        compiler_params=PARAMS,
    )(in_hbm(state), in_hbm(noise))


def unpack_kernel(back, out, held, sems):
    width, each = RING * CELLS // PIECES, RING // PIECES
    copies = []
    for piece in range(PIECES):
        for rank in range(piece * each, (piece + 1) * each):
            held[:, :, rank * CELLS : (rank + 1) * CELLS] = back[rank]
        lanes = pl.ds(piece * width, width)
        copy = pltpu.make_async_copy(held.at[:, :, lanes], out.at[:, :, lanes], sems.at[piece])
        copy.start()
        copies.append(copy)
    for copy in copies:
        copy.wait()


def unpack(back):
    return pl.pallas_call(
        unpack_kernel,
        out_shape=pltpu.HBM((VARIABLES, LOCAL_MEMBERS, RING * CELLS), BF16),
        in_specs=[VMEM],
        out_specs=HBM,
        scratch_shapes=[
            pltpu.VMEM((VARIABLES, LOCAL_MEMBERS, RING * CELLS), BF16),
            pltpu.SemaphoreType.DMA((PIECES,)),
        ],
        compiler_params=PARAMS,
    )(back)


def in_hbm(array):
    return pltpu.with_memory_space_constraint(array, pltpu.HBM)


def exchange(packed):
    return lax.all_to_all(packed, "mem", split_axis=0, concat_axis=0, tiled=True)


def on_device(state, obs_noise, obs_values, obs_weights, tapers, pair_source, pair_taper):
    arrived = exchange(pack(state, obs_noise))
    half = (OWNED, MEMBERS, BLOCK)
    place = lax.axis_index("mem")
    index = pair_source[0] - (place * OWNED - RADIUS)
    turn = jnp.where(place % 2 == 1, 2 * OWNED, 0)
    index = jnp.where(index < OWNED, index + turn, jnp.where(index < 2 * OWNED, index, index - turn))
    taper_sums = pl.pallas_call(
        taper_kernel,
        out_shape=shape(OWNED, 3 * OWNED * BLOCK, BLOCK, dtype=F32),
        in_specs=[SMEM, SMEM, VMEM],
        out_specs=VMEM,
        compiler_params=PARAMS,
    )(index, pair_taper[0], tapers)
    edges, anomalies, weighted = pl.pallas_call(
        prepare_kernel,
        out_shape=(shape(2, *half), shape(*half), shape(*half)),
        in_specs=[VMEM] * 4,
        out_specs=(VMEM,) * 3,
        compiler_params=PARAMS,
    )(arrived, obs_values, obs_weights[0], taper_sums)
    across = [(i, i + 1) for i in range(1, RING - 1, 2)]
    across += [(j, i) for i, j in across]
    inside = [(i, i ^ 1) for i in range(RING)]
    far = lax.ppermute(edges, "mem", across)
    mate_anomalies = lax.ppermute(anomalies, "mem", inside)
    mate_weighted = lax.ppermute(weighted, "mem", inside)
    centered = pl.pallas_call(
        center_kernel,
        out_shape=shape(OWNED, MEMBERS, VARIABLES * BLOCK),
        in_specs=[VMEM],
        out_specs=VMEM,
        compiler_params=PARAMS,
    )(arrived)
    partial = pl.pallas_call(
        near_kernel,
        out_shape=shape(OWNED, MEMBERS, VARIABLES * BLOCK, dtype=F32),
        in_specs=[VMEM] * 7,
        out_specs=VMEM,
        compiler_params=PARAMS,
    )(anomalies, mate_anomalies, weighted, mate_weighted, centered, taper_sums, arrived)
    updated = pl.pallas_call(
        far_kernel,
        out_shape=pltpu.HBM((RING, VARIABLES, LOCAL_MEMBERS, CELLS), BF16),
        in_specs=[VMEM] * 4,
        out_specs=HBM,
        scratch_shapes=[
            pltpu.VMEM((RING, VARIABLES, LOCAL_MEMBERS, CELLS), BF16),
            pltpu.SemaphoreType.DMA((PIECES,)),
        ],
        compiler_params=PARAMS,
    )(far, centered, taper_sums, partial)
    return unpack(exchange(updated))


def solution(mesh):
    placed = (
        P(None, "mem", "patch"),
        P("mem", "patch"),
        P("patch", "mem"),
        P("patch", "mem", None, None),
        P(),
        P("patch", "mem", None),
        P("patch", "mem", None),
    )
    return jax.shard_map(
        on_device, mesh=mesh, in_specs=placed, out_specs=P(None, "mem", "patch"), check_vma=False
    )
```

```python
import jax
import jax.numpy as jnp
from jax import lax
from jax.experimental import pallas as pl
from jax.experimental.pallas import tpu as pltpu
from jax.sharding import PartitionSpec as P

MEMBERS = 1024
VARIABLES = 3
BLOCK = 128
RADIUS = 2
PAIRS = 4
OWNED = 2
CELLS = OWNED * BLOCK
LOCAL_MEMBERS = 16
RING = 64
TILES = MEMBERS // BLOCK
PIECES = 4

VMEM = pl.BlockSpec(memory_space=pltpu.VMEM)
SMEM = pl.BlockSpec(memory_space=pltpu.SMEM)
HBM = pl.BlockSpec(memory_space=pltpu.HBM)
PARAMS = pltpu.CompilerParams(vmem_limit_bytes=40 * 1024 * 1024)
BF16 = jnp.bfloat16
F32 = jnp.float32


def shape(*dims, dtype=BF16):
    return jax.ShapeDtypeStruct(dims, dtype)


def prepare_kernel(arrived, obs, weights, tapers, edges, anomalies, weighted):
    del tapers
    first = arrived[:, 0].reshape(MEMBERS, CELLS).astype(F32)
    noise = arrived[:, VARIABLES].reshape(MEMBERS, CELLS).astype(F32)
    mean = jnp.sum(first, axis=0, keepdims=True) * (1.0 / MEMBERS)
    anomaly = (first - mean).astype(BF16)
    innovation = (obs[...] + noise - first).astype(BF16)
    for block in range(OWNED):
        lanes = slice(block * BLOCK, (block + 1) * BLOCK)
        for tile in range(TILES):
            rows = slice(tile * BLOCK, (tile + 1) * BLOCK)
            turned = anomaly[rows, lanes].T
            edges[0, block, rows] = turned
            anomalies[block, rows] = turned
        product = lax.dot_general(
            innovation[:, lanes],
            weights[block],
            (((1,), (1,)), ((), ())),
            preferred_element_type=F32,
        ).astype(BF16)
        edges[1, block] = product
        weighted[block] = product


def member_columns(part, block):
    return jnp.concatenate(
        [part[block, tile * BLOCK : (tile + 1) * BLOCK] for tile in range(TILES)], axis=1
    )


def center_kernel(arrived, centered):
    for variable in range(VARIABLES):
        wide = arrived[:, variable].reshape(MEMBERS, CELLS).astype(F32)
        mean = jnp.sum(wide, axis=0, keepdims=True) * (1.0 / MEMBERS)
        anomaly = (wide - mean).astype(BF16)
        for block in range(OWNED):
            lanes = slice(block * BLOCK, (block + 1) * BLOCK)
            centered[block, :, variable * BLOCK : (variable + 1) * BLOCK] = anomaly[:, lanes]


def taper_kernel(index, taper_at, table, tapers):
    for block in range(OWNED):
        tiles = [table[taper_at[block, pair]].T * (1.0 / (MEMBERS - 1)) for pair in range(PAIRS)]
        for source in range(3 * OWNED):
            total = jnp.zeros((BLOCK, BLOCK), F32)
            for pair in range(PAIRS):
                total += tiles[pair] * jnp.where(index[block, pair] == source, 1.0, 0.0)
            tapers[block, source * BLOCK : (source + 1) * BLOCK] = total


def localized_part(left, centered, tapers):
    covariance = jnp.dot(left, centered, preferred_element_type=F32)
    return (jnp.concatenate([tapers] * VARIABLES, axis=1) * covariance).astype(BF16)


def near_kernel(own, mate, own_weighted, mate_weighted, centered, tapers, arrived, partial):
    depth, owners = MEMBERS // PIECES, RING // PIECES
    left = jnp.concatenate(
        [member_columns(part, block) for part in (own, mate) for block in range(OWNED)], axis=0
    )
    localized = [
        localized_part(left, centered[block], tapers[block, OWNED * BLOCK :])
        for block in range(OWNED)
    ]
    for piece in range(PIECES):
        rows = slice(piece * depth, (piece + 1) * depth)
        held = slice(piece * owners, (piece + 1) * owners)
        right = jnp.concatenate(
            [part[b, rows] for part in (own_weighted, mate_weighted) for b in range(OWNED)], axis=1
        )
        for block in range(OWNED):
            lanes = slice(block * BLOCK, (block + 1) * BLOCK)
            step = jnp.dot(right, localized[block], preferred_element_type=F32)
            for v in range(VARIABLES):
                base = arrived[held, v, :, lanes].reshape(depth, BLOCK).astype(F32)
                columns = slice(v * BLOCK, (v + 1) * BLOCK)
                partial[block, rows, columns] = base + step[:, columns]


def far_kernel(core, across, centered, tapers, partial, updated, out, out_sems):
    depth, owners = MEMBERS // PIECES, RING // PIECES
    both, one = core[0], 1 - core[0]
    first = jnp.concatenate([member_columns(across.at[0], b) for b in range(OWNED)], axis=0)
    wide = localized_part(first, centered[both], tapers[both, : OWNED * BLOCK])
    near_rows = pl.ds(pl.multiple_of(one * BLOCK, BLOCK), BLOCK)
    narrow = localized_part(member_columns(across.at[0], one), centered[one], tapers[one, near_rows])
    leaving = []
    for piece in range(PIECES):
        rows = slice(piece * depth, (piece + 1) * depth)
        held = slice(piece * owners, (piece + 1) * owners)
        right = jnp.concatenate([across[1, block, rows] for block in range(OWNED)], axis=1)
        for block, weighted, localized in ((both, right, wide), (one, across[1, one, rows], narrow)):
            lanes = pl.ds(pl.multiple_of(block * BLOCK, BLOCK), BLOCK)
            step = jnp.dot(weighted, localized, preferred_element_type=F32)
            result = (partial[block, rows] + step).astype(BF16)
            for v in range(VARIABLES):
                columns = slice(v * BLOCK, (v + 1) * BLOCK)
                out[held, v, :, lanes] = result[:, columns].reshape(owners, LOCAL_MEMBERS, BLOCK)
        part = pl.ds(piece * owners, owners)
        copy = pltpu.make_async_copy(out.at[part], updated.at[part], out_sems.at[piece])
        copy.start()
        leaving.append(copy)
    for copy in leaving:
        copy.wait()


def pack_kernel(state, noise, packed, held, out, sems, out_sems):
    width, each = RING * CELLS // PIECES, RING // PIECES
    entering = []
    for piece in range(PIECES):
        lanes = pl.ds(piece * width, width)
        pair = (
            pltpu.make_async_copy(
                state.at[:, :, lanes], held.at[pl.ds(0, VARIABLES), :, lanes], sems.at[2 * piece]
            ),
            pltpu.make_async_copy(
                noise.at[:, lanes], held.at[VARIABLES, :, lanes], sems.at[2 * piece + 1]
            ),
        )
        for copy in pair:
            copy.start()
        entering.append(pair)
    leaving = []
    for piece in range(PIECES):
        for copy in entering[piece]:
            copy.wait()
        for rank in range(piece * each, (piece + 1) * each):
            out[rank] = held[:, :, rank * CELLS : (rank + 1) * CELLS]
        part = pl.ds(piece * each, each)
        copy = pltpu.make_async_copy(out.at[part], packed.at[part], out_sems.at[piece])
        copy.start()
        leaving.append(copy)
    for copy in leaving:
        copy.wait()


def pack(state, noise):
    count = VARIABLES + 1
    return pl.pallas_call(
        pack_kernel,
        out_shape=pltpu.HBM((RING, count, LOCAL_MEMBERS, CELLS), BF16),
        in_specs=[HBM] * 2,
        out_specs=HBM,
        scratch_shapes=[
            pltpu.VMEM((count, LOCAL_MEMBERS, RING * CELLS), BF16),
            pltpu.VMEM((RING, count, LOCAL_MEMBERS, CELLS), BF16),
            pltpu.SemaphoreType.DMA((2 * PIECES,)),
            pltpu.SemaphoreType.DMA((PIECES,)),
        ],
        compiler_params=PARAMS,
    )(in_hbm(state), in_hbm(noise))


def unpack_kernel(back, out, held, sems):
    width, each = RING * CELLS // PIECES, RING // PIECES
    copies = []
    for piece in range(PIECES):
        for rank in range(piece * each, (piece + 1) * each):
            held[:, :, rank * CELLS : (rank + 1) * CELLS] = back[rank]
        lanes = pl.ds(piece * width, width)
        copy = pltpu.make_async_copy(held.at[:, :, lanes], out.at[:, :, lanes], sems.at[piece])
        copy.start()
        copies.append(copy)
    for copy in copies:
        copy.wait()


def unpack(back):
    return pl.pallas_call(
        unpack_kernel,
        out_shape=pltpu.HBM((VARIABLES, LOCAL_MEMBERS, RING * CELLS), BF16),
        in_specs=[VMEM],
        out_specs=HBM,
        scratch_shapes=[
            pltpu.VMEM((VARIABLES, LOCAL_MEMBERS, RING * CELLS), BF16),
            pltpu.SemaphoreType.DMA((PIECES,)),
        ],
        compiler_params=PARAMS,
    )(back)


def in_hbm(array):
    return pltpu.with_memory_space_constraint(array, pltpu.HBM)


def exchange(packed):
    return lax.all_to_all(packed, "mem", split_axis=0, concat_axis=0, tiled=True)


def on_device(state, obs_noise, obs_values, obs_weights, tapers, pair_source, pair_taper):
    arrived = exchange(pack(state, obs_noise))
    half = (OWNED, MEMBERS, BLOCK)
    place = lax.axis_index("mem")
    index = pair_source[0] - (place * OWNED - RADIUS)
    turn = jnp.where(place % 2 == 1, 2 * OWNED, 0)
    index = jnp.where(index < OWNED, index + turn, jnp.where(index < 2 * OWNED, index, index - turn))
    taper_sums = pl.pallas_call(
        taper_kernel,
        out_shape=shape(OWNED, 3 * OWNED * BLOCK, BLOCK, dtype=F32),
        in_specs=[SMEM, SMEM, VMEM],
        out_specs=VMEM,
        compiler_params=PARAMS,
    )(index, pair_taper[0], tapers)
    edges, anomalies, weighted = pl.pallas_call(
        prepare_kernel,
        out_shape=(shape(2, *half), shape(*half), shape(*half)),
        in_specs=[VMEM] * 4,
        out_specs=(VMEM,) * 3,
        compiler_params=PARAMS,
    )(arrived, obs_values, obs_weights[0], taper_sums)
    across = [(i, i + 1) for i in range(1, RING - 1, 2)]
    across += [(j, i) for i, j in across]
    inside = [(i, i ^ 1) for i in range(RING)]
    far = lax.ppermute(edges, "mem", across)
    mate_anomalies = lax.ppermute(anomalies, "mem", inside)
    mate_weighted = lax.ppermute(weighted, "mem", inside)
    centered = pl.pallas_call(
        center_kernel,
        out_shape=shape(OWNED, MEMBERS, VARIABLES * BLOCK),
        in_specs=[VMEM],
        out_specs=VMEM,
        compiler_params=PARAMS,
    )(arrived)
    partial = pl.pallas_call(
        near_kernel,
        out_shape=shape(OWNED, MEMBERS, VARIABLES * BLOCK, dtype=F32),
        in_specs=[VMEM] * 7,
        out_specs=VMEM,
        compiler_params=PARAMS,
    )(anomalies, mate_anomalies, weighted, mate_weighted, centered, taper_sums, arrived)
    updated = pl.pallas_call(
        far_kernel,
        out_shape=pltpu.HBM((RING, VARIABLES, LOCAL_MEMBERS, CELLS), BF16),
        in_specs=[SMEM] + [VMEM] * 4,
        out_specs=HBM,
        scratch_shapes=[
            pltpu.VMEM((RING, VARIABLES, LOCAL_MEMBERS, CELLS), BF16),
            pltpu.SemaphoreType.DMA((PIECES,)),
        ],
        compiler_params=PARAMS,
    )((place % 2).reshape(1), far, centered, taper_sums, partial)
    return unpack(exchange(updated))


def solution(mesh):
    placed = (
        P(None, "mem", "patch"),
        P("mem", "patch"),
        P("patch", "mem"),
        P("patch", "mem", None, None),
        P(),
        P("patch", "mem", None),
        P("patch", "mem", None),
    )
    return jax.shard_map(
        on_device, mesh=mesh, in_specs=placed, out_specs=P(None, "mem", "patch"), check_vma=False
    )
```

```python
import jax
import jax.numpy as jnp
from jax import lax
from jax.experimental import pallas as pl
from jax.experimental.pallas import tpu as pltpu
from jax.sharding import PartitionSpec as P

MEMBERS = 1024
VARIABLES = 3
BLOCK = 128
RADIUS = 2
PAIRS = 4
OWNED = 2
CELLS = OWNED * BLOCK
LOCAL_MEMBERS = 16
RING = 64
TILES = MEMBERS // BLOCK
PIECES = 2

VMEM = pl.BlockSpec(memory_space=pltpu.VMEM)
SMEM = pl.BlockSpec(memory_space=pltpu.SMEM)
HBM = pl.BlockSpec(memory_space=pltpu.HBM)
PARAMS = pltpu.CompilerParams(vmem_limit_bytes=40 * 1024 * 1024)
BF16 = jnp.bfloat16
F32 = jnp.float32


def shape(*dims, dtype=BF16):
    return jax.ShapeDtypeStruct(dims, dtype)


def prepare_kernel(arrived, obs, weights, tapers, edges, anomalies, weighted):
    del tapers
    first = arrived[:, 0].reshape(MEMBERS, CELLS).astype(F32)
    noise = arrived[:, VARIABLES].reshape(MEMBERS, CELLS).astype(F32)
    mean = jnp.sum(first, axis=0, keepdims=True) * (1.0 / MEMBERS)
    anomaly = (first - mean).astype(BF16)
    innovation = (obs[...] + noise - first).astype(BF16)
    for block in range(OWNED):
        lanes = slice(block * BLOCK, (block + 1) * BLOCK)
        for tile in range(TILES):
            rows = slice(tile * BLOCK, (tile + 1) * BLOCK)
            turned = anomaly[rows, lanes].T
            edges[0, block, rows] = turned
            anomalies[block, rows] = turned
        product = lax.dot_general(
            innovation[:, lanes],
            weights[block],
            (((1,), (1,)), ((), ())),
            preferred_element_type=F32,
        ).astype(BF16)
        edges[1, block] = product
        weighted[block] = product


def member_columns(part, block):
    return jnp.concatenate(
        [part[block, tile * BLOCK : (tile + 1) * BLOCK] for tile in range(TILES)], axis=1
    )


def center_kernel(arrived, centered):
    for variable in range(VARIABLES):
        wide = arrived[:, variable].reshape(MEMBERS, CELLS).astype(F32)
        mean = jnp.sum(wide, axis=0, keepdims=True) * (1.0 / MEMBERS)
        anomaly = (wide - mean).astype(BF16)
        for block in range(OWNED):
            lanes = slice(block * BLOCK, (block + 1) * BLOCK)
            centered[block, :, variable * BLOCK : (variable + 1) * BLOCK] = anomaly[:, lanes]


def taper_kernel(index, taper_at, table, tapers):
    for block in range(OWNED):
        tiles = [table[taper_at[block, pair]].T * (1.0 / (MEMBERS - 1)) for pair in range(PAIRS)]
        for source in range(3 * OWNED):
            total = jnp.zeros((BLOCK, BLOCK), F32)
            for pair in range(PAIRS):
                total += tiles[pair] * jnp.where(index[block, pair] == source, 1.0, 0.0)
            tapers[block, source * BLOCK : (source + 1) * BLOCK] = total


def localized_part(left, centered, tapers):
    covariance = jnp.dot(left, centered, preferred_element_type=F32)
    return (jnp.concatenate([tapers] * VARIABLES, axis=1) * covariance).astype(BF16)


def near_kernel(own, mate, own_weighted, mate_weighted, centered, tapers, arrived, partial):
    depth, owners = MEMBERS // PIECES, RING // PIECES
    left = jnp.concatenate(
        [member_columns(part, block) for part in (own, mate) for block in range(OWNED)], axis=0
    )
    localized = [
        localized_part(left, centered[block], tapers[block, OWNED * BLOCK :])
        for block in range(OWNED)
    ]
    for piece in range(PIECES):
        rows = slice(piece * depth, (piece + 1) * depth)
        held = slice(piece * owners, (piece + 1) * owners)
        right = jnp.concatenate(
            [part[b, rows] for part in (own_weighted, mate_weighted) for b in range(OWNED)], axis=1
        )
        for block in range(OWNED):
            lanes = slice(block * BLOCK, (block + 1) * BLOCK)
            step = jnp.dot(right, localized[block], preferred_element_type=F32)
            for v in range(VARIABLES):
                base = arrived[held, v, :, lanes].reshape(depth, BLOCK).astype(F32)
                columns = slice(v * BLOCK, (v + 1) * BLOCK)
                partial[block, rows, columns] = base + step[:, columns]


def far_kernel(core, across, centered, tapers, partial, updated, out, out_sems):
    depth, owners = MEMBERS // PIECES, RING // PIECES
    both, one = core[0], 1 - core[0]
    first = jnp.concatenate([member_columns(across.at[0], b) for b in range(OWNED)], axis=0)
    wide = localized_part(first, centered[both], tapers[both, : OWNED * BLOCK])
    near_rows = pl.ds(pl.multiple_of(one * BLOCK, BLOCK), BLOCK)
    narrow = localized_part(member_columns(across.at[0], one), centered[one], tapers[one, near_rows])
    leaving = []
    for piece in range(PIECES):
        rows = slice(piece * depth, (piece + 1) * depth)
        held = slice(piece * owners, (piece + 1) * owners)
        right = jnp.concatenate([across[1, block, rows] for block in range(OWNED)], axis=1)
        for block, weighted, localized in ((both, right, wide), (one, across[1, one, rows], narrow)):
            lanes = pl.ds(pl.multiple_of(block * BLOCK, BLOCK), BLOCK)
            step = jnp.dot(weighted, localized, preferred_element_type=F32)
            result = (partial[block, rows] + step).astype(BF16)
            for v in range(VARIABLES):
                columns = slice(v * BLOCK, (v + 1) * BLOCK)
                out[held, v, :, lanes] = result[:, columns].reshape(owners, LOCAL_MEMBERS, BLOCK)
        part = pl.ds(piece * owners, owners)
        copy = pltpu.make_async_copy(out.at[part], updated.at[part], out_sems.at[piece])
        copy.start()
        leaving.append(copy)
    for copy in leaving:
        copy.wait()


def pack_kernel(state, noise, packed, held, out, sems, out_sems):
    width, each = RING * CELLS // PIECES, RING // PIECES
    entering = []
    for piece in range(PIECES):
        lanes = pl.ds(piece * width, width)
        pair = (
            pltpu.make_async_copy(
                state.at[:, :, lanes], held.at[pl.ds(0, VARIABLES), :, lanes], sems.at[2 * piece]
            ),
            pltpu.make_async_copy(
                noise.at[:, lanes], held.at[VARIABLES, :, lanes], sems.at[2 * piece + 1]
            ),
        )
        for copy in pair:
            copy.start()
        entering.append(pair)
    leaving = []
    for piece in range(PIECES):
        for copy in entering[piece]:
            copy.wait()
        for rank in range(piece * each, (piece + 1) * each):
            out[rank] = held[:, :, rank * CELLS : (rank + 1) * CELLS]
        part = pl.ds(piece * each, each)
        copy = pltpu.make_async_copy(out.at[part], packed.at[part], out_sems.at[piece])
        copy.start()
        leaving.append(copy)
    for copy in leaving:
        copy.wait()


def pack(state, noise):
    count = VARIABLES + 1
    return pl.pallas_call(
        pack_kernel,
        out_shape=pltpu.HBM((RING, count, LOCAL_MEMBERS, CELLS), BF16),
        in_specs=[HBM] * 2,
        out_specs=HBM,
        scratch_shapes=[
            pltpu.VMEM((count, LOCAL_MEMBERS, RING * CELLS), BF16),
            pltpu.VMEM((RING, count, LOCAL_MEMBERS, CELLS), BF16),
            pltpu.SemaphoreType.DMA((2 * PIECES,)),
            pltpu.SemaphoreType.DMA((PIECES,)),
        ],
        compiler_params=PARAMS,
    )(in_hbm(state), in_hbm(noise))


def unpack_kernel(back, out, held, sems):
    width, each = RING * CELLS // PIECES, RING // PIECES
    copies = []
    for piece in range(PIECES):
        for rank in range(piece * each, (piece + 1) * each):
            held[:, :, rank * CELLS : (rank + 1) * CELLS] = back[rank]
        lanes = pl.ds(piece * width, width)
        copy = pltpu.make_async_copy(held.at[:, :, lanes], out.at[:, :, lanes], sems.at[piece])
        copy.start()
        copies.append(copy)
    for copy in copies:
        copy.wait()


def unpack(back):
    return pl.pallas_call(
        unpack_kernel,
        out_shape=pltpu.HBM((VARIABLES, LOCAL_MEMBERS, RING * CELLS), BF16),
        in_specs=[VMEM],
        out_specs=HBM,
        scratch_shapes=[
            pltpu.VMEM((VARIABLES, LOCAL_MEMBERS, RING * CELLS), BF16),
            pltpu.SemaphoreType.DMA((PIECES,)),
        ],
        compiler_params=PARAMS,
    )(back)


def in_hbm(array):
    return pltpu.with_memory_space_constraint(array, pltpu.HBM)


def exchange(packed):
    return lax.all_to_all(packed, "mem", split_axis=0, concat_axis=0, tiled=True)


def on_device(state, obs_noise, obs_values, obs_weights, tapers, pair_source, pair_taper):
    arrived = exchange(pack(state, obs_noise))
    half = (OWNED, MEMBERS, BLOCK)
    place = lax.axis_index("mem")
    index = pair_source[0] - (place * OWNED - RADIUS)
    turn = jnp.where(place % 2 == 1, 2 * OWNED, 0)
    index = jnp.where(index < OWNED, index + turn, jnp.where(index < 2 * OWNED, index, index - turn))
    taper_sums = pl.pallas_call(
        taper_kernel,
        out_shape=shape(OWNED, 3 * OWNED * BLOCK, BLOCK, dtype=F32),
        in_specs=[SMEM, SMEM, VMEM],
        out_specs=VMEM,
        compiler_params=PARAMS,
    )(index, pair_taper[0], tapers)
    edges, anomalies, weighted = pl.pallas_call(
        prepare_kernel,
        out_shape=(shape(2, *half), shape(*half), shape(*half)),
        in_specs=[VMEM] * 4,
        out_specs=(VMEM,) * 3,
        compiler_params=PARAMS,
    )(arrived, obs_values, obs_weights[0], taper_sums)
    across = [(i, i + 1) for i in range(1, RING - 1, 2)]
    across += [(j, i) for i, j in across]
    inside = [(i, i ^ 1) for i in range(RING)]
    far = lax.ppermute(edges, "mem", across)
    mate_anomalies = lax.ppermute(anomalies, "mem", inside)
    mate_weighted = lax.ppermute(weighted, "mem", inside)
    centered = pl.pallas_call(
        center_kernel,
        out_shape=shape(OWNED, MEMBERS, VARIABLES * BLOCK),
        in_specs=[VMEM],
        out_specs=VMEM,
        compiler_params=PARAMS,
    )(arrived)
    partial = pl.pallas_call(
        near_kernel,
        out_shape=shape(OWNED, MEMBERS, VARIABLES * BLOCK, dtype=F32),
        in_specs=[VMEM] * 7,
        out_specs=VMEM,
        compiler_params=PARAMS,
    )(anomalies, mate_anomalies, weighted, mate_weighted, centered, taper_sums, arrived)
    updated = pl.pallas_call(
        far_kernel,
        out_shape=pltpu.HBM((RING, VARIABLES, LOCAL_MEMBERS, CELLS), BF16),
        in_specs=[SMEM] + [VMEM] * 4,
        out_specs=HBM,
        scratch_shapes=[
            pltpu.VMEM((RING, VARIABLES, LOCAL_MEMBERS, CELLS), BF16),
            pltpu.SemaphoreType.DMA((PIECES,)),
        ],
        compiler_params=PARAMS,
    )((place % 2).reshape(1), far, centered, taper_sums, partial)
    back = exchange(updated)
    return jnp.transpose(back, (1, 2, 0, 3)).reshape(VARIABLES, LOCAL_MEMBERS, RING * CELLS)


def solution(mesh):
    placed = (
        P(None, "mem", "patch"),
        P("mem", "patch"),
        P("patch", "mem"),
        P("patch", "mem", None, None),
        P(),
        P("patch", "mem", None),
        P("patch", "mem", None),
    )
    return jax.shard_map(
        on_device, mesh=mesh, in_specs=placed, out_specs=P(None, "mem", "patch"), check_vma=False
    )
```
